128 devices in a mesh: blk: 16 (over x_lo, y, core), sp: 8 (over x_hi, z).
Axes of the slice: x: 4 (x_hi: 2, x_lo: 2; x = x_hi * 2 + x_lo), y: 4, z: 4, core: 2. Of those that a mesh axis runs over, the one named last changes fastest.
Arguments:
- query: bfloat16 [33280, 256], P(('blk', 'sp')), may hold values from -6 to 6
- keys: bfloat16 [33280, 256], P(('blk', 'sp')), may hold values from -6 to 6
- values: bfloat16 [33280, 256], P(('blk', 'sp')), may hold values from -6 to 6
Outputs:
- attended: bfloat16 [33280, 256], P(('blk', 'sp'))
The draws below stay inside these ranges and needn't reach their ends.
All inputs are finite; a program needn't handle non-finite values.
Results may differ from the reference program's by a relative error of at most 0.01.
Values may be sent and summed in bfloat16 or wider, within the bound.
A program may use at most 128 MiB of HBM per device.

```python
import jax
import jax.numpy as jnp
from jax import lax

HEAD_DIM = 128
HEADS = 2
TOK_DEV = 260
TOKENS = 33280


def draw_query(key, part):
    key = jax.random.fold_in(key, 11)
    base = jnp.clip(jax.random.normal(key, (TOKENS, HEADS * HEAD_DIM), jnp.float32), -6.0, 6.0)
    return base.astype(jnp.bfloat16)


def draw_keys(key, part):
    key = jax.random.fold_in(key, 23)
    base = jnp.clip(jax.random.normal(key, (TOKENS, HEADS * HEAD_DIM), jnp.float32), -6.0, 6.0)
    return base.astype(jnp.bfloat16)


def levels(key, shape, pieces, least, high):
    def one(dim, blocks):
        heights = jax.random.uniform(jax.random.fold_in(jax.random.fold_in(key, 6), dim), (blocks,), jnp.float32, least / len(pieces), high / len(pieces))
        return jnp.repeat(jnp.exp(heights), shape[dim] // blocks).reshape((-1,) + (1,) * (len(shape) - dim - 1))

    level = one(*pieces[0])
    for cut in pieces[1:]:
        level = level * one(*cut)
    return level


def normal_values(stream_key, shape, width, most, shards=(), kind=jnp.bfloat16):
    values = width * jax.random.normal(stream_key, shape, jnp.float32)
    if shards:
        values = values * levels(stream_key, shape, shards, -0.22, 0.18)
    return jnp.clip(values, -most, most).astype(kind)


def setup_inputs(seed: int = 0) -> dict:
    arg_keys = jax.random.split(jax.random.key(seed), 4)
    return {
        "query": draw_query(jax.random.fold_in(arg_keys[3], 71), 0),
        "keys": draw_keys(jax.random.fold_in(arg_keys[3], 71), 0),
        "values": normal_values(arg_keys[2], (TOKENS, HEADS * HEAD_DIM), 1.0, 6.0, ((0, 128),)),
    }


def reference(query, keys, values):
    head_size = query.shape[1] // HEADS
    score_scale = head_size ** -0.5
    keys_wide = keys.astype(jnp.float32).reshape(TOKENS, HEADS, head_size)
    values_wide = values.astype(jnp.float32).reshape(TOKENS, HEADS, head_size)

    def attend(query_block):
        scores = jnp.einsum('qhd,khd->hqk', query_block.astype(jnp.float32), keys_wide) * score_scale
        row_max = jnp.max(scores, axis=-1, keepdims=True)
        weights = jnp.exp(scores - row_max)
        totals = jnp.sum(weights, axis=-1)
        weights_low = lax.optimization_barrier(weights.astype(jnp.bfloat16))
        mixed_sum = jnp.einsum('hqk,khd->qhd', weights_low.astype(jnp.float32), values_wide)
        return (mixed_sum / jnp.transpose(totals)[:, :, None]).astype(jnp.bfloat16)

    blocks = query.reshape(TOKENS // TOK_DEV, TOK_DEV, HEADS, head_size)
    return lax.map(attend, blocks).reshape(TOKENS, HEADS * head_size)
```

```python
import jax
import jax.numpy as jnp
from jax import lax
from jax.experimental import pallas as pl
from jax.experimental.pallas import tpu as pltpu
from jax.sharding import PartitionSpec as P

MESH = pl.DeviceIdType.MESH
HEADS = 2
HEAD = 128
ROWS = 260
FULL = 256
PAD = 272
PAIR = 2 * PAD
LOG2E = 1.4426950408889634
FACTOR = HEAD**-0.5 * LOG2E

NEAR = (0, 1, 2, 3, 4, 5, 8, 9)
FAR = (6, 7, 10, 11, 12, 13, 14, 15)
SECOND = ((1, 1, 0), (2, 1, 0), (2, 2, 0), (1, 4, 1), (0, 4, 1), (0, 2, 1))
THIRD = ((2, 3, 0), (0, 6, 1))


def place():
    blk, sp = lax.axis_index("blk"), lax.axis_index("sp")
    return (2 * (sp // 4) + blk // 8, (blk // 2) % 4, sp % 4), blk % 2


def device(chip, core):
    x, y, z = chip
    return ((x % 2) * 8 + y * 2 + core, (x // 2) * 4 + z)


def pair_even(a):
    return a + 1 - 2 * (a % 2)


def pair_odd(a):
    return (a + 3 + 2 * (a % 2)) % 4


def neighbour(chip, axis, pair):
    return tuple(pair(a) if n == axis else a for n, a in enumerate(chip))


def kernel(
    q_ref, k_ref, v_ref, out_ref,
    kv_mine, q_mine, kv_held, q_held, peak, mixed, wide_a, wide_b, top_a, top_b,
    part, lse, got, got_lse,
    kv_send, kv_recv, q_send, q_recv, part_send, part_recv, lse_send, lse_recv,
):
    chip, core = place()
    sibling = device(chip, 1 - core)

    def stage(ref, store, head):
        cols = pl.ds(pl.multiple_of(head * HEAD, HEAD), HEAD)
        store(0, FULL, ref[0:FULL, cols])
        store(FULL, PAD, ref[0 : PAD - FULL, cols])
        store(FULL, ROWS, ref[FULL:ROWS, cols])

    def into(ref, lanes, slot=None):
        def store(lo, hi, rows):
            if slot is None:
                ref[lo:hi, lanes] = rows
            else:
                ref[slot, lo:hi, lanes] = rows

        return store

    low, high = slice(0, HEAD), slice(HEAD, 2 * HEAD)
    stage(q_ref, into(q_held, low, core), core)
    stage(k_ref, into(kv_held, low, core), core)
    stage(v_ref, into(kv_held, high, core), core)
    stage(q_ref, into(q_mine, low), 1 - core)
    stage(k_ref, into(kv_mine, low), 1 - core)
    stage(v_ref, into(kv_mine, high), 1 - core)
    pads = jnp.zeros((PAD - ROWS, HEAD), jnp.bfloat16)
    kv_held[core, ROWS:PAD, high] = pads
    kv_mine[ROWS:PAD, high] = pads

    barrier = pltpu.get_barrier_semaphore()
    pl.semaphore_signal(barrier, inc=1, device_id=sibling, device_id_type=MESH)
    for pair in (pair_odd, pair_even):
        for axis in range(3):
            pl.semaphore_signal(
                barrier, inc=1, device_id=device(neighbour(chip, axis, pair), core), device_id_type=MESH
            )
    pl.semaphore_wait(barrier, 7)

    sends = []

    def send(kind, axis, offset, c):
        held, send_sem, recv_sem, pair = kind
        slot, there = 2 * offset + c, 2 * (offset + 2**axis) + c
        copy = pltpu.make_async_remote_copy(
            held.at[slot], held.at[there], send_sem.at[there], recv_sem.at[there],
            device_id=device(neighbour(chip, axis, pair), core), device_id_type=MESH,
        )
        copy.start()
        sends.append(copy)

    def cross(kind, mine):
        held, send_sem, recv_sem, pair = kind
        copy = pltpu.make_async_remote_copy(
            mine, held.at[core], send_sem.at[0], recv_sem.at[core], device_id=sibling, device_id_type=MESH
        )
        copy.start()
        sends.append(copy)

    def arrive(kind, slot):
        held, send_sem, recv_sem, pair = kind
        pltpu.make_async_copy(held.at[slot], held.at[slot], recv_sem.at[slot]).wait()

    q_kind = (q_held, q_send, q_recv, pair_odd)
    kv_kind = (kv_held, kv_send, kv_recv, pair_even)
    cross(q_kind, q_mine)
    cross(kv_kind, kv_mine)
    for axis in range(3):
        send(q_kind, axis, 0, core)
        send(kv_kind, axis, 0, core)
    arrive(q_kind, 1 - core)
    for axis in range(3):
        send(q_kind, axis, 0, 1 - core)
    arrive(kv_kind, 1 - core)
    for axis in range(3):
        send(kv_kind, axis, 0, 1 - core)
    seen = set()

    def forward(kind, steps):
        for axis, offset, c in steps:
            if (id(kind), offset, c) not in seen:
                seen.add((id(kind), offset, c))
                arrive(kind, 2 * offset + c)
            send(kind, axis, offset, c)

    def rest(kind, slots):
        for slot in slots:
            if slot > 1 and (id(kind), slot // 2, slot % 2) not in seen:
                seen.add((id(kind), slot // 2, slot % 2))
                arrive(kind, slot)

    forward(q_kind, SECOND)
    forward(kv_kind, SECOND)
    forward(q_kind, THIRD)
    rest(q_kind, range(16))
    rest(kv_kind, NEAR)

    def keys_of(slots, tails):
        rows = [kv_held[s, 0:FULL, low] for s in slots]
        if tails:
            rows += [kv_held[s, FULL:PAD, low] for s in range(16)]
        keys = jnp.concatenate(rows, axis=0)
        return jnp.concatenate([keys, keys], axis=1)

    def values_of(slots, tails):
        rows = [kv_held[s, 0:FULL, high] for s in slots]
        ones = jnp.ones((FULL * len(slots), HEAD), jnp.bfloat16)
        if tails:
            rows += [kv_held[s, FULL:PAD, high] for s in range(16)]
            row = lax.broadcasted_iota(jnp.int32, (16 * (PAD - FULL), HEAD), 0)
            real = jnp.where(row % (PAD - FULL) < ROWS - FULL, 1.0, 0.0).astype(jnp.bfloat16)
            ones = jnp.concatenate([ones, real], axis=0)
        return jnp.concatenate([jnp.concatenate(rows, axis=0), ones], axis=1)

    def rows_of(t):
        return pl.ds(pl.multiple_of(t * PAIR, 16), PAIR)

    def score(t, slots, tails, wide, top):
        q = q_held[pl.ds(2 * t, 2)].reshape(PAIR, HEAD).astype(jnp.float32) * FACTOR
        q_high = q.astype(jnp.bfloat16)
        q_low = (q - q_high.astype(jnp.float32)).astype(jnp.bfloat16)
        s = lax.dot_general(
            jnp.concatenate([q_high, q_low], axis=1), keys_of(slots, tails),
            (((1,), (1,)), ((), ())), preferred_element_type=jnp.float32,
        )
        width = s.shape[1]
        wide[:, 0:width] = s
        most = s[:, 0:HEAD]
        for j in range(HEAD, width, HEAD):
            most = jnp.maximum(most, s[:, j : j + HEAD])
        top[...] = jnp.broadcast_to(jnp.max(most, axis=1, keepdims=True), (PAIR, HEAD))

    def mix(slots, tails, wide, peaks):
        width = FULL * len(slots) + (16 * (PAD - FULL) if tails else 0)
        weights = jnp.exp2(wide[:, 0:width] - jnp.concatenate([peaks] * (width // HEAD), axis=1))
        return jnp.dot(weights.astype(jnp.bfloat16), values_of(slots, tails), preferred_element_type=jnp.float32)

    def first(t, wide, top):
        peaks = top[...]
        peak[rows_of(t), :] = peaks
        mixed[rows_of(t), :] = mix(NEAR, False, wide, peaks)

    def last(t, wide, top):
        before = peak[rows_of(t), :]
        peaks = jnp.maximum(before, top[...])
        shrink = jnp.exp2(before - peaks)
        total = mixed[rows_of(t), :] * jnp.concatenate([shrink, shrink], axis=1) + mix(FAR, True, wide, peaks)
        sums = total[:, HEAD:]
        part[pl.ds(2 * t, 2)] = (total[:, 0:HEAD] / sums).astype(jnp.bfloat16).reshape(2, PAD, HEAD)
        logs = peaks + jnp.log2(sums)
        pick = jnp.where(lax.broadcasted_iota(jnp.int32, (8, HEAD), 1) == 0, 1.0, 0.0)
        for c in range(2):
            lse[2 * t + c, :, 0:PAD] = lax.dot_general(
                pick, logs[c * PAD : (c + 1) * PAD], (((1,), (1,)), ((), ())),
                preferred_element_type=jnp.float32, precision=lax.Precision.HIGHEST,
            )

    def result_copies(t, c):
        owner = tuple(a + ((t // 2**n) % 2) * (pair_odd(a) - a) for n, a in enumerate(chip))
        here, there = 2 * t + c, 2 * t + core
        return [
            pltpu.make_async_remote_copy(
                src.at[here], dst.at[there], send_sem.at[here], recv_sem.at[there],
                device_id=device(owner, c), device_id_type=MESH,
            )
            for src, dst, send_sem, recv_sem in (
                (part, got, part_send, part_recv), (lse, got_lse, lse_send, lse_recv)
            )
        ]

    def post(t):
        for c in range(2):
            for copy in result_copies(t, c):
                copy.start()

    bufs = ((wide_a, top_a), (wide_b, top_b))

    def near_score(t, b):
        score(t, NEAR, False, *bufs[b])

    def far_score(t, b):
        score(t, FAR, True, *bufs[b])

    near_score(0, 0)

    def near_step(i, _):
        near_score(2 * i + 1, 1)
        first(2 * i, *bufs[0])
        near_score(2 * i + 2, 0)
        first(2 * i + 1, *bufs[1])
        return 0

    lax.fori_loop(0, 2, near_step, 0)
    forward(kv_kind, THIRD)
    lax.fori_loop(2, 3, near_step, 0)
    near_score(7, 1)
    first(6, *bufs[0])
    rest(kv_kind, FAR)
    far_score(7, 0)
    first(7, *bufs[1])

    def far_step(i, _):
        t = 7 - 2 * i
        far_score(t - 1, 1)
        last(t, *bufs[0])
        post(t)
        far_score(t - 2, 0)
        last(t - 1, *bufs[1])
        post(t - 1)
        return 0

    lax.fori_loop(0, 3, far_step, 0)
    far_score(0, 1)
    last(1, *bufs[0])
    post(1)
    last(0, *bufs[1])
    crossing = result_copies(0, 1 - core)
    for copy in crossing:
        copy.start()
    got[core] = part[core]
    got_lse[core] = lse[core]

    for slot in range(16):
        for kind, recv in ((got, part_recv), (got_lse, lse_recv)):
            if slot < 2:
                continue
            pltpu.make_async_copy(kind.at[slot], kind.at[slot], recv.at[slot]).wait()
    for kind, recv in ((got, part_recv), (got_lse, lse_recv)):
        pltpu.make_async_copy(kind.at[1 - core], kind.at[1 - core], recv.at[1 - core]).wait()

    which = lax.broadcasted_iota(jnp.int32, (8, PAD), 0)
    for head in range(2):
        logs = got_lse[head, :, 0:PAD]
        for o in range(1, 8):
            logs = jnp.where(which == o, got_lse[2 * o + head, :, 0:PAD], logs)
        shares = jnp.exp2(logs - jnp.max(logs, axis=0, keepdims=True))
        shares = shares / jnp.sum(shares, axis=0, keepdims=True)
        shares = jnp.transpose(shares)
        result = jnp.zeros((PAD, HEAD), jnp.float32)
        for o in range(8):
            result = result + got[2 * o + head].astype(jnp.float32) * shares[:, o : o + 1]
        out_ref[:, head * HEAD : (head + 1) * HEAD] = result[0:ROWS].astype(jnp.bfloat16)

    for copy in sends:
        copy.wait_send()
    for t in range(1, 8):
        for c in range(2):
            for copy in result_copies(t, c):
                copy.wait_send()
    for copy in crossing:
        copy.wait_send()


def local(query, keys, values):
    vmem = pl.BlockSpec(memory_space=pltpu.VMEM)
    shard = (16, PAD, HEAD)
    widest = FULL * len(FAR) + 16 * (PAD - FULL)
    dma = pltpu.SemaphoreType.DMA((16,))
    return pl.pallas_call(
        kernel,
        out_shape=jax.ShapeDtypeStruct((ROWS, HEADS * HEAD), jnp.bfloat16),
        in_specs=[vmem] * 3,
        out_specs=vmem,
        scratch_shapes=[
            pltpu.VMEM((PAD, 2 * HEAD), jnp.bfloat16),
            pltpu.VMEM((PAD, HEAD), jnp.bfloat16),
            pltpu.VMEM((16, PAD, 2 * HEAD), jnp.bfloat16),
            pltpu.VMEM(shard, jnp.bfloat16),
            pltpu.VMEM((16 * PAD, HEAD), jnp.float32),
            pltpu.VMEM((16 * PAD, 2 * HEAD), jnp.float32),
            pltpu.VMEM((PAIR, widest), jnp.float32),
            pltpu.VMEM((PAIR, widest), jnp.float32),
            pltpu.VMEM((PAIR, HEAD), jnp.float32),
            pltpu.VMEM((PAIR, HEAD), jnp.float32),
            pltpu.VMEM(shard, jnp.bfloat16),
            pltpu.VMEM((16, 8, 384), jnp.float32),
            pltpu.VMEM(shard, jnp.bfloat16),
            pltpu.VMEM((16, 8, 384), jnp.float32),
        ]
        + [dma] * 8,
        compiler_params=pltpu.CompilerParams(
            collective_id=0, has_side_effects=True, vmem_limit_bytes=56 * 2**20
        ),
        cost_estimate=pl.CostEstimate(flops=8860000000, bytes_accessed=600000, transcendentals=17300000),
        name="attend",
    )(query, keys, values)


def solution(mesh):
    spec = P(("blk", "sp"), None)
    return jax.shard_map(local, mesh=mesh, in_specs=(spec, spec, spec), out_specs=spec, check_vma=False)
```

```python
import jax
import jax.numpy as jnp
from jax import lax
from jax.experimental import pallas as pl
from jax.experimental.pallas import tpu as pltpu
from jax.sharding import PartitionSpec as P

MESH = pl.DeviceIdType.MESH
HEADS = 2
HEAD = 128
ROWS = 260
FULL = 256
PAD = 272
PAIR = 2 * PAD
LOG2E = 1.4426950408889634
FACTOR = HEAD**-0.5 * LOG2E

NEAR = (0, 1, 2, 3, 4, 5, 8, 9)
FAR = (6, 7, 10, 11, 12, 13, 14, 15)
SECOND = ((1, 1, 0), (2, 1, 0), (2, 2, 0), (1, 4, 1), (0, 4, 1), (0, 2, 1))
THIRD = ((2, 3, 0), (0, 6, 1))


def place():
    blk, sp = lax.axis_index("blk"), lax.axis_index("sp")
    return (2 * (sp // 4) + blk // 8, (blk // 2) % 4, sp % 4), blk % 2


def device(chip, core):
    x, y, z = chip
    return ((x % 2) * 8 + y * 2 + core, (x // 2) * 4 + z)


def pair_even(a):
    return a + 1 - 2 * (a % 2)


def pair_odd(a):
    return (a + 3 + 2 * (a % 2)) % 4


def neighbour(chip, axis, pair):
    return tuple(pair(a) if n == axis else a for n, a in enumerate(chip))


def kernel(
    q_ref, k_ref, v_ref, out_ref,
    kv_mine, q_mine, kv_held, q_held, peak, mixed, wide_a, wide_b, top_a, top_b,
    part, lse, got, got_lse,
    kv_send, kv_recv, q_send, q_recv, part_send, part_recv, lse_send, lse_recv,
):
    chip, core = place()
    sibling = device(chip, 1 - core)

    def stage(ref, store, head):
        cols = pl.ds(pl.multiple_of(head * HEAD, HEAD), HEAD)
        store(0, FULL, ref[0:FULL, cols])
        store(FULL, PAD, ref[0 : PAD - FULL, cols])
        store(FULL, ROWS, ref[FULL:ROWS, cols])

    def into(ref, lanes, slot=None):
        def store(lo, hi, rows):
            if slot is None:
                ref[lo:hi, lanes] = rows
            else:
                ref[slot, lo:hi, lanes] = rows

        return store

    low, high = slice(0, HEAD), slice(HEAD, 2 * HEAD)
    stage(q_ref, into(q_held, low, core), core)
    stage(k_ref, into(kv_held, low, core), core)
    stage(v_ref, into(kv_held, high, core), core)
    stage(q_ref, into(q_mine, low), 1 - core)
    stage(k_ref, into(kv_mine, low), 1 - core)
    stage(v_ref, into(kv_mine, high), 1 - core)
    pads = jnp.zeros((PAD - ROWS, HEAD), jnp.bfloat16)
    kv_held[core, ROWS:PAD, high] = pads
    kv_mine[ROWS:PAD, high] = pads

    barrier = pltpu.get_barrier_semaphore()
    pl.semaphore_signal(barrier, inc=1, device_id=sibling, device_id_type=MESH)
    for pair in (pair_odd, pair_even):
        for axis in range(3):
            pl.semaphore_signal(
                barrier, inc=1, device_id=device(neighbour(chip, axis, pair), core), device_id_type=MESH
            )
    pl.semaphore_wait(barrier, 7)

    sends = []

    def hop(kind, axis, offset, c):
        held, send_sem, recv_sem, pair = kind
        slot, there = 2 * offset + c, 2 * (offset + 2**axis) + c
        return pltpu.make_async_remote_copy(
            held.at[slot], held.at[there], send_sem.at[there], recv_sem.at[there],
            device_id=device(neighbour(chip, axis, pair), core), device_id_type=MESH,
        )

    def send(*what):
        hop(*what).start()
        sends.append(what)

    def cross(kind, mine):
        held, send_sem, recv_sem, pair = kind
        return pltpu.make_async_remote_copy(
            mine, held.at[core], send_sem.at[0], recv_sem.at[core], device_id=sibling, device_id_type=MESH
        )

    def arrive(kind, slot):
        held, send_sem, recv_sem, pair = kind
        pltpu.make_async_copy(held.at[slot], held.at[slot], recv_sem.at[slot]).wait()

    q_kind = (q_held, q_send, q_recv, pair_odd)
    kv_kind = (kv_held, kv_send, kv_recv, pair_even)
    crosses = [cross(q_kind, q_mine), cross(kv_kind, kv_mine)]
    for copy in crosses:
        copy.start()
    for axis in range(3):
        send(q_kind, axis, 0, core)
        send(kv_kind, axis, 0, core)
    arrive(q_kind, 1 - core)
    for axis in range(3):
        send(q_kind, axis, 0, 1 - core)
    arrive(kv_kind, 1 - core)
    for axis in range(3):
        send(kv_kind, axis, 0, 1 - core)
    seen = set()

    def forward(kind, steps):
        for axis, offset, c in steps:
            if (id(kind), offset, c) not in seen:
                seen.add((id(kind), offset, c))
                arrive(kind, 2 * offset + c)
            send(kind, axis, offset, c)

    def rest(kind, slots):
        for slot in slots:
            if slot > 1 and (id(kind), slot // 2, slot % 2) not in seen:
                seen.add((id(kind), slot // 2, slot % 2))
                arrive(kind, slot)

    forward(q_kind, SECOND)
    forward(kv_kind, SECOND)
    rest(kv_kind, NEAR)
    rest(q_kind, NEAR)

    def keys_of(slots, tails):
        rows = [kv_held[s, 0:FULL, low] for s in slots]
        if tails:
            rows += [kv_held[s, FULL:PAD, low] for s in range(16)]
        keys = jnp.concatenate(rows, axis=0)
        return jnp.concatenate([keys, keys], axis=1)

    def values_of(slots, tails):
        rows = [kv_held[s, 0:FULL, high] for s in slots]
        ones = jnp.ones((FULL * len(slots), HEAD), jnp.bfloat16)
        if tails:
            rows += [kv_held[s, FULL:PAD, high] for s in range(16)]
            row = lax.broadcasted_iota(jnp.int32, (16 * (PAD - FULL), HEAD), 0)
            real = jnp.where(row % (PAD - FULL) < ROWS - FULL, 1.0, 0.0).astype(jnp.bfloat16)
            ones = jnp.concatenate([ones, real], axis=0)
        return jnp.concatenate([jnp.concatenate(rows, axis=0), ones], axis=1)

    def rows_of(t):
        return pl.ds(pl.multiple_of(t * PAIR, 16), PAIR)

    def score(t, slots, tails, wide, top):
        q = q_held[pl.ds(2 * t, 2)].reshape(PAIR, HEAD).astype(jnp.float32) * FACTOR
        q_high = q.astype(jnp.bfloat16)
        q_low = (q - q_high.astype(jnp.float32)).astype(jnp.bfloat16)
        s = lax.dot_general(
            jnp.concatenate([q_high, q_low], axis=1), keys_of(slots, tails),
            (((1,), (1,)), ((), ())), preferred_element_type=jnp.float32,
        )
        width = s.shape[1]
        wide[:, 0:width] = s
        most = s[:, 0:HEAD]
        for j in range(HEAD, width, HEAD):
            most = jnp.maximum(most, s[:, j : j + HEAD])
        top[...] = jnp.broadcast_to(jnp.max(most, axis=1, keepdims=True), (PAIR, HEAD))

    def mix(slots, tails, wide, peaks):
        width = FULL * len(slots) + (16 * (PAD - FULL) if tails else 0)
        weights = jnp.exp2(wide[:, 0:width] - jnp.concatenate([peaks] * (width // HEAD), axis=1))
        return jnp.dot(weights.astype(jnp.bfloat16), values_of(slots, tails), preferred_element_type=jnp.float32)

    def across(column):
        lane = lax.broadcasted_iota(jnp.int32, (HEAD, HEAD), 1)
        diagonal = lane == lax.broadcasted_iota(jnp.int32, (HEAD, HEAD), 0)
        row = lax.broadcasted_iota(jnp.int32, (8, HEAD), 0)
        result = jnp.zeros((8, HEAD), jnp.float32)
        for n, lo in enumerate(range(0, PAD, HEAD)):
            rows = min(HEAD, PAD - lo)
            line = jnp.sum(jnp.where(diagonal[:rows], column[lo : lo + rows], 0.0), axis=0, keepdims=True)
            result = jnp.where(row == n, line, result)
        return result

    def first(t, wide, top):
        peaks = top[...]
        peak[rows_of(t), :] = peaks
        mixed[rows_of(t), :] = mix(NEAR, False, wide, peaks)

    def last(t, wide, top):
        before = peak[rows_of(t), :]
        peaks = jnp.maximum(before, top[...])
        shrink = jnp.exp2(before - peaks)
        total = mixed[rows_of(t), :] * jnp.concatenate([shrink, shrink], axis=1) + mix(FAR, True, wide, peaks)
        sums = total[:, HEAD:]
        part[pl.ds(2 * t, 2)] = (total[:, 0:HEAD] / sums).astype(jnp.bfloat16).reshape(2, PAD, HEAD)
        logs = peaks + jnp.log2(sums)
        for c in range(2):
            lse[2 * t + c] = across(logs[c * PAD : (c + 1) * PAD])

    def result_copies(t, c):
        owner = tuple(a + ((t // 2**n) % 2) * (pair_odd(a) - a) for n, a in enumerate(chip))
        here, there = 2 * t + c, 2 * t + core
        return [
            pltpu.make_async_remote_copy(
                src.at[here], dst.at[there], send_sem.at[here], recv_sem.at[there],
                device_id=device(owner, c), device_id_type=MESH,
            )
            for src, dst, send_sem, recv_sem in (
                (part, got, part_send, part_recv), (lse, got_lse, lse_send, lse_recv)
            )
        ]

    def post(t):
        for c in range(2):
            for copy in result_copies(t, c):
                copy.start()

    bufs = ((wide_a, top_a), (wide_b, top_b))

    def near_score(t, b):
        score(t, NEAR, False, *bufs[b])

    def far_score(t, b):
        score(t, FAR, True, *bufs[b])

    def near_tile(p):
        return jnp.where(p == 3, 4, jnp.where(p == 4, 3, p))

    near_score(0, 0)

    def near_step(i, _):
        @pl.when(i == 1)
        def _():
            forward(q_kind, THIRD)
            rest(q_kind, (6, 7))

        @pl.when(i == 2)
        def _():
            rest(q_kind, range(14))
            forward(kv_kind, THIRD[:1])

        near_score(near_tile(2 * i + 1), 1)
        first(near_tile(2 * i), *bufs[0])
        near_score(near_tile(2 * i + 2), 0)
        first(near_tile(2 * i + 1), *bufs[1])
        return 0

    lax.fori_loop(0, 3, near_step, 0)
    forward(kv_kind, THIRD[1:])
    rest(q_kind, range(16))
    near_score(7, 1)
    first(6, *bufs[0])
    rest(kv_kind, FAR)
    far_score(7, 0)
    first(7, *bufs[1])

    def far_step(i, _):
        t = 7 - 2 * i
        far_score(t - 1, 1)
        last(t, *bufs[0])
        post(t)
        far_score(t - 2, 0)
        last(t - 1, *bufs[1])
        post(t - 1)
        return 0

    lax.fori_loop(0, 3, far_step, 0)
    far_score(0, 1)
    last(1, *bufs[0])
    post(1)
    last(0, *bufs[1])
    crossing = result_copies(0, 1 - core)
    for copy in crossing:
        copy.start()
    got[core] = part[core]
    got_lse[core] = lse[core]

    for slot in range(16):
        for kind, recv in ((got, part_recv), (got_lse, lse_recv)):
            if slot < 2:
                continue
            pltpu.make_async_copy(kind.at[slot], kind.at[slot], recv.at[slot]).wait()
    for kind, recv in ((got, part_recv), (got_lse, lse_recv)):
        pltpu.make_async_copy(kind.at[1 - core], kind.at[1 - core], recv.at[1 - core]).wait()

    which = lax.broadcasted_iota(jnp.int32, (8, HEAD), 0)
    for head in range(2):
        logs = [got_lse[2 * o + head] for o in range(8)]
        most = logs[0]
        for o in range(1, 8):
            most = jnp.maximum(most, logs[o])
        shares = [jnp.exp2(x - most) for x in logs]
        every = shares[0]
        for o in range(1, 8):
            every = every + shares[o]
        shares = [x / every for x in shares]
        columns = []
        for n in range(3):
            lines = jnp.broadcast_to(shares[0][n : n + 1], (8, HEAD))
            for o in range(1, 8):
                lines = jnp.where(which == o, shares[o][n : n + 1], lines)
            columns.append(jnp.transpose(lines))
        shares = jnp.concatenate(columns, axis=0)[0:PAD]
        result = jnp.zeros((PAD, HEAD), jnp.float32)
        for o in range(8):
            result = result + got[2 * o + head].astype(jnp.float32) * shares[:, o : o + 1]
        out_ref[:, head * HEAD : (head + 1) * HEAD] = result[0:ROWS].astype(jnp.bfloat16)

    for copy in crosses:
        copy.wait_send()
    for what in sends:
        hop(*what).wait_send()
    for t in range(1, 8):
        for c in range(2):
            for copy in result_copies(t, c):
                copy.wait_send()
    for copy in crossing:
        copy.wait_send()


def local(query, keys, values):
    vmem = pl.BlockSpec(memory_space=pltpu.VMEM)
    shard = (16, PAD, HEAD)
    widest = FULL * len(FAR) + 16 * (PAD - FULL)
    dma = pltpu.SemaphoreType.DMA((16,))
    return pl.pallas_call(
        kernel,
        out_shape=jax.ShapeDtypeStruct((ROWS, HEADS * HEAD), jnp.bfloat16),
        in_specs=[vmem] * 3,
        out_specs=vmem,
        scratch_shapes=[
            pltpu.VMEM((PAD, 2 * HEAD), jnp.bfloat16),
            pltpu.VMEM((PAD, HEAD), jnp.bfloat16),
            pltpu.VMEM((16, PAD, 2 * HEAD), jnp.bfloat16),
            pltpu.VMEM(shard, jnp.bfloat16),
            pltpu.VMEM((16 * PAD, HEAD), jnp.float32),
            pltpu.VMEM((16 * PAD, 2 * HEAD), jnp.float32),
            pltpu.VMEM((PAIR, widest), jnp.float32),
            pltpu.VMEM((PAIR, widest), jnp.float32),
            pltpu.VMEM((PAIR, HEAD), jnp.float32),
            pltpu.VMEM((PAIR, HEAD), jnp.float32),
            pltpu.VMEM(shard, jnp.bfloat16),
            pltpu.VMEM((16, 8, HEAD), jnp.float32),
            pltpu.VMEM(shard, jnp.bfloat16),
            pltpu.VMEM((16, 8, HEAD), jnp.float32),
        ]
        + [dma] * 8,
        compiler_params=pltpu.CompilerParams(
            collective_id=0, has_side_effects=True, vmem_limit_bytes=56 * 2**20
        ),
        cost_estimate=pl.CostEstimate(flops=8860000000, bytes_accessed=600000, transcendentals=17300000),
        name="attend",
    )(query, keys, values)


def solution(mesh):
    spec = P(("blk", "sp"), None)
    return jax.shard_map(local, mesh=mesh, in_specs=(spec, spec, spec), out_specs=spec, check_vma=False)
```

```python
import jax
import jax.numpy as jnp
from jax import lax
from jax.experimental import pallas as pl
from jax.experimental.pallas import tpu as pltpu
from jax.sharding import PartitionSpec as P

MESH = pl.DeviceIdType.MESH
HEADS = 2
HEAD = 128
ROWS = 260
FULL = 256
PAD = 272
PART = 264
PAIR = 2 * PART
LOG2E = 1.4426950408889634
FACTOR = HEAD**-0.5 * LOG2E

NEAR = (0, 1, 2, 3, 4, 5, 8, 9)
FAR = (6, 7, 10, 11, 12, 13, 14, 15)

def place():
    blk, sp = lax.axis_index("blk"), lax.axis_index("sp")
    return (2 * (sp // 4) + blk // 8, (blk // 2) % 4, sp % 4), blk % 2


def device(chip, core):
    x, y, z = chip
    return ((x % 2) * 8 + y * 2 + core, (x // 2) * 4 + z)


def pair_even(a):
    return a + 1 - 2 * (a % 2)


def pair_odd(a):
    return (a + 3 + 2 * (a % 2)) % 4


def neighbour(chip, axes, pair):
    return tuple(pair(a) if n in axes else a for n, a in enumerate(chip))


def kernel(
    q_ref, k_ref, v_ref, out_ref,
    kv_mine, q_mine, kv_held, q_held, peak, mixed, wide_a, wide_b, top_a, top_b,
    part, got,
    kv_send, kv_recv, q_send, q_recv, part_send, part_recv,
):
    chip, core = place()
    sibling = device(chip, 1 - core)

    barrier = pltpu.get_barrier_semaphore()
    pl.semaphore_signal(barrier, inc=1, device_id=sibling, device_id_type=MESH)
    for pair in (pair_odd, pair_even):
        for axis in range(3):
            pl.semaphore_signal(
                barrier, inc=1, device_id=device(neighbour(chip, (axis,), pair), core), device_id_type=MESH
            )

    def stage(ref, store, head):
        cols = pl.ds(pl.multiple_of(head * HEAD, HEAD), HEAD)
        store(0, FULL, ref[0:FULL, cols])
        store(FULL, PAD, ref[0 : PAD - FULL, cols])
        store(FULL, ROWS, ref[FULL:ROWS, cols])

    def into(ref, lanes, slot=None):
        def store(lo, hi, rows):
            if slot is None:
                ref[lo:hi, lanes] = rows
            else:
                ref[slot, lo:hi, lanes] = rows

        return store

    low, high = slice(0, HEAD), slice(HEAD, 2 * HEAD)
    stage(q_ref, into(q_held, low, core), core)
    stage(k_ref, into(kv_held, low, core), core)
    stage(v_ref, into(kv_held, high, core), core)
    stage(q_ref, into(q_mine, low), 1 - core)
    stage(k_ref, into(kv_mine, low), 1 - core)
    stage(v_ref, into(kv_mine, high), 1 - core)
    pads = jnp.zeros((PAD - ROWS, HEAD), jnp.bfloat16)
    kv_held[core, ROWS:PAD, high] = pads
    kv_mine[ROWS:PAD, high] = pads

    pl.semaphore_wait(barrier, 7)

    sends = []
    early, late = core, 1 - core

    def hop(kind, axes, offset, c):
        held, send_sem, recv_sem, pair = kind
        slot, there = 2 * offset + c, 2 * (offset + sum(2**axis for axis in axes)) + c
        return pltpu.make_async_remote_copy(
            held.at[slot], held.at[there], send_sem.at[there], recv_sem.at[there],
            device_id=device(neighbour(chip, axes, pair), core), device_id_type=MESH,
        )

    def send(*what):
        hop(*what).start()
        sends.append(what)

    def cross(kind, mine):
        held, send_sem, recv_sem, pair = kind
        return pltpu.make_async_remote_copy(
            mine, held.at[core], send_sem.at[core], recv_sem.at[core], device_id=sibling, device_id_type=MESH
        )

    def arrive(kind, offset, c):
        held, send_sem, recv_sem, pair = kind
        slot = 2 * offset + c
        pltpu.make_async_copy(held.at[slot], held.at[slot], recv_sem.at[slot]).wait()

    def own(kind, c):
        for axis in range(3):
            send(kind, (axis,), 0, c)

    def forward(kind, c):
        for axis in range(3):
            arrive(kind, 2**axis, c)
        for axis in range(3):
            send(kind, (axis,), 2 ** ((axis + 1) % 3), c)

    def corner(kind):
        arrive(kind, 6, early)
        send(kind, (0,), 6, early)
        send(kind, (1, 2), 1, late)

    q_kind = (q_held, q_send, q_recv, pair_odd)
    kv_kind = (kv_held, kv_send, kv_recv, pair_even)
    crosses = [cross(q_kind, q_mine), cross(kv_kind, kv_mine)]
    for copy in crosses:
        copy.start()
    own(q_kind, early)
    own(kv_kind, early)
    arrive(q_kind, 0, late)
    own(q_kind, late)
    arrive(kv_kind, 0, late)
    own(kv_kind, late)
    forward(q_kind, early)
    forward(kv_kind, early)
    forward(q_kind, late)
    forward(kv_kind, late)

    def keys_of(slots, tails):
        rows = [kv_held[s, 0:FULL, low] for s in slots]
        if tails:
            rows += [kv_held[s, FULL:PAD, low] for s in range(16)]
        keys = jnp.concatenate(rows, axis=0)
        return jnp.concatenate([keys, keys], axis=1)

    def values_of(slots, tails):
        rows = [kv_held[s, 0:FULL, high] for s in slots]
        ones = jnp.ones((FULL * len(slots), HEAD), jnp.bfloat16)
        if tails:
            rows += [kv_held[s, FULL:PAD, high] for s in range(16)]
            row = lax.broadcasted_iota(jnp.int32, (16 * (PAD - FULL), HEAD), 0)
            real = jnp.where(row % (PAD - FULL) < ROWS - FULL, 1.0, 0.0).astype(jnp.bfloat16)
            ones = jnp.concatenate([ones, real], axis=0)
        return jnp.concatenate([jnp.concatenate(rows, axis=0), ones], axis=1)

    def rows_of(t):
        return pl.ds(pl.multiple_of(t * PAIR, 16), PAIR)

    def score(t, slots, tails, wide, top):
        q = jnp.concatenate([q_held[2 * t + c].astype(jnp.float32)[0:PART] for c in range(2)], axis=0) * FACTOR
        q_high = q.astype(jnp.bfloat16)
        q_low = (q - q_high.astype(jnp.float32)).astype(jnp.bfloat16)
        s = lax.dot_general(
            jnp.concatenate([q_high, q_low], axis=1), keys_of(slots, tails),
            (((1,), (1,)), ((), ())), preferred_element_type=jnp.float32,
        )
        width = s.shape[1]
        wide[:, 0:width] = s
        most = s[:, 0:HEAD]
        for j in range(HEAD, width, HEAD):
            most = jnp.maximum(most, s[:, j : j + HEAD])
        top[...] = jnp.broadcast_to(jnp.max(most, axis=1, keepdims=True), (PAIR, HEAD))

    def mix(slots, tails, wide, peaks):
        width = FULL * len(slots) + (16 * (PAD - FULL) if tails else 0)
        weights = jnp.exp2(wide[:, 0:width] - jnp.concatenate([peaks] * (width // HEAD), axis=1))
        return jnp.dot(weights.astype(jnp.bfloat16), values_of(slots, tails), preferred_element_type=jnp.float32)

    def with_logs(block, column):
        lane = lax.broadcasted_iota(jnp.int32, (HEAD, HEAD), 1)
        diagonal = lane == lax.broadcasted_iota(jnp.int32, (HEAD, HEAD), 0)
        row = lax.broadcasted_iota(jnp.int32, (8, HEAD), 0)
        lines = jnp.zeros((8, HEAD), jnp.float32)
        for n, lo in enumerate(range(0, PART, HEAD)):
            rows = min(HEAD, PART - lo)
            line = jnp.sum(jnp.where(diagonal[:rows], column[lo : lo + rows], 0.0), axis=0, keepdims=True)
            lines = jnp.where(row % 3 == n, line, lines)
        one = lines.astype(jnp.bfloat16).astype(jnp.float32)
        two = (lines - one).astype(jnp.bfloat16).astype(jnp.float32)
        three = lines - one - two
        logs = jnp.where(row < 3, one, jnp.where(row < 6, two, three))
        third = jnp.broadcast_to(three[2:3], (8, HEAD))
        return jnp.concatenate([jnp.where(row == 4, third, block), logs], axis=0)

    def logs_of(tile):
        row = lax.broadcasted_iota(jnp.int32, (8, HEAD), 0)
        block, logs = tile[0:8], tile[8:16]
        three = jnp.where(row == 2, pltpu.roll(block, 6, 0), pltpu.roll(logs, 2, 0))
        return logs + pltpu.roll(logs, 5, 0) + three

    def first(t, wide, top):
        peaks = top[...]
        peak[rows_of(t), :] = peaks
        mixed[rows_of(t), :] = mix(NEAR, False, wide, peaks)

    def last(t, wide, top):
        before = peak[rows_of(t), :]
        peaks = jnp.maximum(before, top[...])
        shrink = jnp.exp2(before - peaks)
        total = mixed[rows_of(t), :] * jnp.concatenate([shrink, shrink], axis=1) + mix(FAR, True, wide, peaks)
        sums = total[:, HEAD:]
        result = total[:, 0:HEAD] / sums
        logs = peaks + jnp.log2(sums)
        for c in range(2):
            mine = result[c * PART : (c + 1) * PART]
            part[2 * t + c, 0:FULL] = mine[0:FULL].astype(jnp.bfloat16)
            end = with_logs(mine[FULL:PART], logs[c * PART : (c + 1) * PART])
            part[2 * t + c, FULL:PAD] = end.astype(jnp.bfloat16)

    def result_copy(t, c):
        owner = tuple(a + ((t // 2**n) % 2) * (pair_odd(a) - a) for n, a in enumerate(chip))
        here, there = 2 * t + c, 2 * t + core
        return pltpu.make_async_remote_copy(
            part.at[here], got.at[there], part_send.at[here], part_recv.at[there],
            device_id=device(owner, c), device_id_type=MESH,
        )

    def post(t):
        for c in range(2):
            result_copy(t, c).start()

    bufs = ((wide_a, top_a), (wide_b, top_b))

    def near_score(t, b):
        score(t, NEAR, False, *bufs[b])

    def far_score(t, b):
        score(t, FAR, True, *bufs[b])

    def near_tile(p):
        return jnp.where(p == 2, 4, jnp.where(p == 3, 3, p + 1))

    near_score(near_tile(0), 0)
    corner(q_kind)

    def near_step(i, _):
        @pl.when(i == 1)
        def _():
            corner(kv_kind)
            arrive(q_kind, 3, early)
            arrive(q_kind, 3, late)

        @pl.when(i == 2)
        def _():
            arrive(q_kind, 6, late)

        near_score(near_tile(2 * i + 1), 1)
        first(near_tile(2 * i), *bufs[0])

        @pl.when(i == 1)
        def _():
            arrive(q_kind, 5, early)
            arrive(q_kind, 5, late)

        @pl.when(i == 2)
        def _():
            arrive(q_kind, 7, early)
            arrive(q_kind, 7, late)

        near_score(near_tile(2 * i + 2), 0)
        first(near_tile(2 * i + 1), *bufs[1])
        return 0

    lax.fori_loop(0, 3, near_step, 0)
    for offset in (3, 5, 6, 7):
        if offset != 6:
            arrive(kv_kind, offset, early)
        arrive(kv_kind, offset, late)
    far_score(7, 1)
    first(7, *bufs[0])

    def far_step(i, _):
        t = 7 - 2 * i
        far_score(t - 1, 0)
        last(t, *bufs[1])
        post(t)
        far_score(t - 2, 1)
        last(t - 1, *bufs[0])
        post(t - 1)
        return 0

    lax.fori_loop(0, 3, far_step, 0)
    near_score(0, 0)
    last(1, *bufs[1])
    post(1)
    far_score(0, 1)
    first(0, *bufs[0])
    last(0, *bufs[1])
    crossing = result_copy(0, 1 - core)
    crossing.start()
    got[core] = part[core]

    for slot in range(2, 16):
        pltpu.make_async_copy(got.at[slot], got.at[slot], part_recv.at[slot]).wait()
    pltpu.make_async_copy(got.at[1 - core], got.at[1 - core], part_recv.at[1 - core]).wait()

    which = lax.broadcasted_iota(jnp.int32, (8, HEAD), 0)
    for head in range(2):
        logs = [logs_of(got[2 * o + head, FULL:PAD].astype(jnp.float32)) for o in range(8)]
        most = logs[0]
        for o in range(1, 8):
            most = jnp.maximum(most, logs[o])
        shares = [jnp.exp2(x - most) for x in logs]
        every = shares[0]
        for o in range(1, 8):
            every = every + shares[o]
        shares = [x / every for x in shares]
        columns = []
        for n in range(3):
            lines = jnp.broadcast_to(shares[0][n : n + 1], (8, HEAD))
            for o in range(1, 8):
                lines = jnp.where(which == o, shares[o][n : n + 1], lines)
            columns.append(jnp.transpose(lines))
        shares = jnp.concatenate(columns, axis=0)[0:PART]
        result = jnp.zeros((PART, HEAD), jnp.float32)
        for o in range(8):
            result = result + got[2 * o + head].astype(jnp.float32)[0:PART] * shares[:, o : o + 1]
        out_ref[:, head * HEAD : (head + 1) * HEAD] = result[0:ROWS].astype(jnp.bfloat16)

    for copy in crosses:
        copy.wait_send()
    for what in sends:
        hop(*what).wait_send()
    for t in range(1, 8):
        for c in range(2):
            result_copy(t, c).wait_send()
    crossing.wait_send()


def local(query, keys, values):
    vmem = pl.BlockSpec(memory_space=pltpu.VMEM)
    shard = (16, PAD, HEAD)
    widest = FULL * len(FAR) + 16 * (PAD - FULL)
    dma = pltpu.SemaphoreType.DMA((16,))
    return pl.pallas_call(
        kernel,
        out_shape=jax.ShapeDtypeStruct((ROWS, HEADS * HEAD), jnp.bfloat16),
        in_specs=[vmem] * 3,
        out_specs=vmem,
        scratch_shapes=[
            pltpu.VMEM((PAD, 2 * HEAD), jnp.bfloat16),
            pltpu.VMEM((PAD, HEAD), jnp.bfloat16),
            pltpu.VMEM((16, PAD, 2 * HEAD), jnp.bfloat16),
            pltpu.VMEM(shard, jnp.bfloat16),
            pltpu.VMEM((8 * PAIR, HEAD), jnp.float32),
            pltpu.VMEM((8 * PAIR, 2 * HEAD), jnp.float32),
            pltpu.VMEM((PAIR, widest), jnp.float32),
            pltpu.VMEM((PAIR, widest), jnp.float32),
            pltpu.VMEM((PAIR, HEAD), jnp.float32),
            pltpu.VMEM((PAIR, HEAD), jnp.float32),
            pltpu.VMEM(shard, jnp.bfloat16),
            pltpu.VMEM(shard, jnp.bfloat16),
        ]
        + [dma] * 6,
        compiler_params=pltpu.CompilerParams(
            collective_id=0, has_side_effects=True, vmem_limit_bytes=56 * 2**20
        ),
        cost_estimate=pl.CostEstimate(flops=8860000000, bytes_accessed=600000, transcendentals=17300000),
        name="attend",
    )(query, keys, values)


def solution(mesh):
    spec = P(("blk", "sp"), None)
    return jax.shard_map(local, mesh=mesh, in_specs=(spec, spec, spec), out_specs=spec, check_vma=False)
```

```python
import jax
import jax.numpy as jnp
from jax import lax
from jax.experimental import pallas as pl
from jax.experimental.pallas import tpu as pltpu
from jax.sharding import PartitionSpec as P

MESH = pl.DeviceIdType.MESH
HEADS = 2
HEAD = 128
ROWS = 260
FULL = 256
PAD = 272
PART = 264
TAIL = 128
PAIR = 2 * PART
LOG2E = 1.4426950408889634
FACTOR = HEAD**-0.5 * LOG2E

NEAR = (0, 1, 2, 3, 4, 5, 8, 9)
FAR = (6, 7, 10, 11, 12, 13, 14, 15)

def place():
    blk, sp = lax.axis_index("blk"), lax.axis_index("sp")
    return (2 * (sp // 4) + blk // 8, (blk // 2) % 4, sp % 4), blk % 2


def device(chip, core):
    x, y, z = chip
    return ((x % 2) * 8 + y * 2 + core, (x // 2) * 4 + z)


def pair_even(a):
    return a + 1 - 2 * (a % 2)


def pair_odd(a):
    return (a + 3 + 2 * (a % 2)) % 4


def neighbour(chip, axes, pair):
    return tuple(pair(a) if n in axes else a for n, a in enumerate(chip))


def kernel(
    q_ref, k_ref, v_ref, out_ref,
    kv_mine, q_mine, kv_held, q_held, peak, mixed, wide_a, wide_b, top_a, top_b,
    part, got,
    kv_send, kv_recv, q_send, q_recv, part_send, part_recv,
):
    chip, core = place()
    sibling = device(chip, 1 - core)

    barrier = pltpu.get_barrier_semaphore()
    pl.semaphore_signal(barrier, inc=1, device_id=sibling, device_id_type=MESH)
    diagonal = device(neighbour(chip, (1, 2), pair_even), core)
    pl.semaphore_signal(barrier, inc=1, device_id=diagonal, device_id_type=MESH)
    for pair in (pair_odd, pair_even):
        for axis in range(3):
            pl.semaphore_signal(
                barrier, inc=1, device_id=device(neighbour(chip, (axis,), pair), core), device_id_type=MESH
            )

    def stage(ref, store, head):
        cols = pl.ds(pl.multiple_of(head * HEAD, HEAD), HEAD)
        store(0, FULL, ref[0:FULL, cols])
        store(FULL, PAD, ref[0 : PAD - FULL, cols])
        store(FULL, ROWS, ref[FULL:ROWS, cols])

    def into(ref, lanes, slot=None):
        def store(lo, hi, rows):
            if slot is None:
                ref[lo:hi, lanes] = rows
            else:
                ref[slot, lo:hi, lanes] = rows

        return store

    low, high = slice(0, HEAD), slice(HEAD, 2 * HEAD)
    spot = chip[0] % 2 + 2 * (chip[1] % 2)
    mine = lax.broadcasted_iota(jnp.int32, (PAD - FULL, HEAD), 0) // (ROWS - FULL) == spot

    def stage_keys(ref, store, head):
        cols = pl.ds(pl.multiple_of(head * HEAD, HEAD), HEAD)
        store(0, FULL, ref[0:FULL, cols])
        rest = ref[FULL:ROWS, cols].astype(jnp.float32)
        for lo in range(0, PAD - FULL, ROWS - FULL):
            top_a[lo : lo + ROWS - FULL, :] = rest
        store(FULL, PAD, jnp.where(mine, top_a[0 : PAD - FULL, :], 0.0).astype(jnp.bfloat16))

    stage(q_ref, into(q_held, low, core), core)
    stage_keys(k_ref, into(kv_held, low, core), core)
    stage_keys(v_ref, into(kv_held, high, core), core)
    stage(q_ref, into(q_mine, low), 1 - core)
    stage_keys(k_ref, into(kv_mine, low), 1 - core)
    stage_keys(v_ref, into(kv_mine, high), 1 - core)

    pl.semaphore_wait(barrier, 8)

    sends = []
    early, late = core, 1 - core

    def hop(kind, axes, offset, c):
        held, send_sem, recv_sem, pair = kind
        slot, there = 2 * offset + c, 2 * (offset + sum(2**axis for axis in axes)) + c
        return pltpu.make_async_remote_copy(
            held.at[slot], held.at[there], send_sem.at[there], recv_sem.at[there],
            device_id=device(neighbour(chip, axes, pair), core), device_id_type=MESH,
        )

    def send(*what):
        hop(*what).start()
        sends.append(what)

    def cross(kind, mine):
        held, send_sem, recv_sem, pair = kind
        return pltpu.make_async_remote_copy(
            mine, held.at[core], send_sem.at[core], recv_sem.at[core], device_id=sibling, device_id_type=MESH
        )

    def arrive(kind, offset, c):
        held, send_sem, recv_sem, pair = kind
        slot = 2 * offset + c
        pltpu.make_async_copy(held.at[slot], held.at[slot], recv_sem.at[slot]).wait()

    def own(kind, c):
        for axis in range(3):
            send(kind, (axis,), 0, c)

    def forward(kind, c):
        for axis in range(3):
            arrive(kind, 2**axis, c)
        for axis in range(3):
            send(kind, (axis,), 2 ** ((axis + 1) % 3), c)

    def corner(kind, c):
        if c is early:
            arrive(kind, 6, c)
            send(kind, (0,), 6, c)
        else:
            send(kind, (1, 2), 1, c)

    q_kind = (q_held, q_send, q_recv, pair_odd)
    kv_kind = (kv_held, kv_send, kv_recv, pair_even)
    crosses = [cross(kv_kind, kv_mine), cross(q_kind, q_mine)]
    own(kv_kind, early)
    for copy in crosses:
        copy.start()
    own(q_kind, early)
    arrive(kv_kind, 0, late)
    own(kv_kind, late)
    arrive(q_kind, 0, late)
    own(q_kind, late)
    forward(q_kind, early)
    forward(kv_kind, early)
    forward(q_kind, late)
    forward(kv_kind, late)
    corner(kv_kind, late)

    def packed(lanes):
        tiles = []
        for z in range(2):
            for c in range(2):
                a, b, d, e = (kv_held[2 * (4 * z + o) + c, FULL:PAD, lanes] for o in range(4))
                tiles.append((a + b) + (d + e))
        return jnp.concatenate(tiles, axis=0)

    def keys_of(slots, tails):
        rows = [kv_held[s, 0:FULL, low] for s in slots]
        if tails:
            rows += [packed(low)] * 2
        keys = jnp.concatenate(rows, axis=0)
        return jnp.concatenate([keys, keys], axis=1)

    def values_of(slots, tails):
        rows = [kv_held[s, 0:FULL, high] for s in slots]
        ones = jnp.ones((FULL * len(slots), HEAD), jnp.bfloat16)
        if tails:
            rows += [packed(high), jnp.zeros((TAIL // 2, HEAD), jnp.bfloat16)]
            half = jnp.ones((TAIL // 2, HEAD), jnp.bfloat16)
            ones = jnp.concatenate([ones, half, jnp.zeros_like(half)], axis=0)
        return jnp.concatenate([jnp.concatenate(rows, axis=0), ones], axis=1)

    def rows_of(t):
        return pl.ds(pl.multiple_of(t * PAIR, 16), PAIR)

    def score(t, slots, tails, wide, top):
        q = jnp.concatenate([q_held[2 * t + c].astype(jnp.float32)[0:PART] for c in range(2)], axis=0) * FACTOR
        q_high = q.astype(jnp.bfloat16)
        q_low = (q - q_high.astype(jnp.float32)).astype(jnp.bfloat16)
        s = lax.dot_general(
            jnp.concatenate([q_high, q_low], axis=1), keys_of(slots, tails),
            (((1,), (1,)), ((), ())), preferred_element_type=jnp.float32,
        )
        width = s.shape[1]
        wide[:, 0:width] = s
        most = s[:, 0:HEAD]
        for j in range(HEAD, width, HEAD):
            most = jnp.maximum(most, s[:, j : j + HEAD])
        top[...] = jnp.broadcast_to(jnp.max(most, axis=1, keepdims=True), (PAIR, HEAD))

    def mix(slots, tails, wide, peaks):
        width = FULL * len(slots) + (TAIL if tails else 0)
        weights = jnp.exp2(wide[:, 0:width] - jnp.concatenate([peaks] * (width // HEAD), axis=1))
        return jnp.dot(weights.astype(jnp.bfloat16), values_of(slots, tails), preferred_element_type=jnp.float32)

    def with_logs(block, column):
        lane = lax.broadcasted_iota(jnp.int32, (HEAD, HEAD), 1)
        diagonal = lane == lax.broadcasted_iota(jnp.int32, (HEAD, HEAD), 0)
        row = lax.broadcasted_iota(jnp.int32, (8, HEAD), 0)
        lines = jnp.zeros((8, HEAD), jnp.float32)
        for n, lo in enumerate(range(0, PART, HEAD)):
            rows = min(HEAD, PART - lo)
            line = jnp.sum(jnp.where(diagonal[:rows], column[lo : lo + rows], 0.0), axis=0, keepdims=True)
            lines = jnp.where(row % 3 == n, line, lines)
        one = lines.astype(jnp.bfloat16).astype(jnp.float32)
        two = (lines - one).astype(jnp.bfloat16).astype(jnp.float32)
        three = lines - one - two
        logs = jnp.where(row < 3, one, jnp.where(row < 6, two, three))
        third = jnp.broadcast_to(three[2:3], (8, HEAD))
        return jnp.concatenate([jnp.where(row == 4, third, block), logs], axis=0)

    def logs_of(tile):
        row = lax.broadcasted_iota(jnp.int32, (8, HEAD), 0)
        block, logs = tile[0:8], tile[8:16]
        three = jnp.where(row == 2, pltpu.roll(block, 6, 0), pltpu.roll(logs, 2, 0))
        return logs + pltpu.roll(logs, 5, 0) + three

    def first(t, wide, top):
        peaks = top[...]
        peak[rows_of(t), :] = peaks
        mixed[rows_of(t), :] = mix(NEAR, False, wide, peaks)

    def last(t, wide, top):
        before = peak[rows_of(t), :]
        peaks = jnp.maximum(before, top[...])
        shrink = jnp.exp2(before - peaks)
        total = mixed[rows_of(t), :] * jnp.concatenate([shrink, shrink], axis=1) + mix(FAR, True, wide, peaks)
        sums = total[:, HEAD:]
        result = total[:, 0:HEAD] / sums
        logs = peaks + jnp.log2(sums)
        for c in range(2):
            mine = result[c * PART : (c + 1) * PART]
            part[2 * t + c, 0:FULL] = mine[0:FULL].astype(jnp.bfloat16)
            end = with_logs(mine[FULL:PART], logs[c * PART : (c + 1) * PART])
            part[2 * t + c, FULL:PAD] = end.astype(jnp.bfloat16)

    def result_copy(t, c):
        owner = tuple(a + ((t // 2**n) % 2) * (pair_odd(a) - a) for n, a in enumerate(chip))
        here, there = 2 * t + c, 2 * t + core
        return pltpu.make_async_remote_copy(
            part.at[here], got.at[there], part_send.at[here], part_recv.at[there],
            device_id=device(owner, c), device_id_type=MESH,
        )

    def post(t):
        for c in range(2):
            result_copy(t, c).start()

    bufs = ((wide_a, top_a), (wide_b, top_b))

    def near_score(t, b):
        score(t, NEAR, False, *bufs[b])

    def far_score(t, b):
        score(t, FAR, True, *bufs[b])

    def near_tile(p):
        return jnp.where(p == 2, 4, jnp.where(p == 3, 3, p + 1))

    near_score(near_tile(0), 0)
    corner(q_kind, early)
    corner(q_kind, late)

    def near_step(i, _):
        @pl.when(i == 1)
        def _():
            corner(kv_kind, early)
            arrive(q_kind, 3, early)
            arrive(q_kind, 3, late)

        @pl.when(i == 2)
        def _():
            arrive(q_kind, 6, late)

        near_score(near_tile(2 * i + 1), 1)
        first(near_tile(2 * i), *bufs[0])

        @pl.when(i == 1)
        def _():
            arrive(q_kind, 5, early)
            arrive(q_kind, 5, late)

        @pl.when(i == 2)
        def _():
            arrive(q_kind, 7, early)
            arrive(q_kind, 7, late)

        near_score(near_tile(2 * i + 2), 0)
        first(near_tile(2 * i + 1), *bufs[1])
        return 0

    lax.fori_loop(0, 3, near_step, 0)
    for offset in (3, 5, 6, 7):
        if offset != 6:
            arrive(kv_kind, offset, early)
        arrive(kv_kind, offset, late)
    far_score(7, 1)
    first(7, *bufs[0])

    def far_step(i, _):
        t = 7 - 2 * i
        far_score(t - 1, 0)
        last(t, *bufs[1])
        post(t)
        far_score(t - 2, 1)
        last(t - 1, *bufs[0])
        post(t - 1)
        return 0

    lax.fori_loop(0, 3, far_step, 0)
    near_score(0, 0)
    last(1, *bufs[1])
    post(1)
    far_score(0, 1)
    first(0, *bufs[0])
    last(0, *bufs[1])
    crossing = result_copy(0, 1 - core)
    crossing.start()
    got[core] = part[core]

    for slot in range(2, 16):
        pltpu.make_async_copy(got.at[slot], got.at[slot], part_recv.at[slot]).wait()
    pltpu.make_async_copy(got.at[1 - core], got.at[1 - core], part_recv.at[1 - core]).wait()

    which = lax.broadcasted_iota(jnp.int32, (8, HEAD), 0)
    for head in range(2):
        logs = [logs_of(got[2 * o + head, FULL:PAD].astype(jnp.float32)) for o in range(8)]
        most = logs[0]
        for o in range(1, 8):
            most = jnp.maximum(most, logs[o])
        shares = [jnp.exp2(x - most) for x in logs]
        every = shares[0]
        for o in range(1, 8):
            every = every + shares[o]
        shares = [x / every for x in shares]
        columns = []
        for n in range(3):
            lines = jnp.broadcast_to(shares[0][n : n + 1], (8, HEAD))
            for o in range(1, 8):
                lines = jnp.where(which == o, shares[o][n : n + 1], lines)
            columns.append(jnp.transpose(lines))
        shares = jnp.concatenate(columns, axis=0)[0:PART]
        result = jnp.zeros((PART, HEAD), jnp.float32)
        for o in range(8):
            result = result + got[2 * o + head].astype(jnp.float32)[0:PART] * shares[:, o : o + 1]
        out_ref[:, head * HEAD : (head + 1) * HEAD] = result[0:ROWS].astype(jnp.bfloat16)

    for copy in crosses:
        copy.wait_send()
    for what in sends:
        hop(*what).wait_send()
    for t in range(1, 8):
        for c in range(2):
            result_copy(t, c).wait_send()
    crossing.wait_send()


def local(query, keys, values):
    vmem = pl.BlockSpec(memory_space=pltpu.VMEM)
    shard = (16, PAD, HEAD)
    widest = FULL * len(FAR) + TAIL
    dma = pltpu.SemaphoreType.DMA((16,))
    return pl.pallas_call(
        kernel,
        out_shape=jax.ShapeDtypeStruct((ROWS, HEADS * HEAD), jnp.bfloat16),
        in_specs=[vmem] * 3,
        out_specs=vmem,
        scratch_shapes=[
            pltpu.VMEM((PAD, 2 * HEAD), jnp.bfloat16),
            pltpu.VMEM((PAD, HEAD), jnp.bfloat16),
            pltpu.VMEM((16, PAD, 2 * HEAD), jnp.bfloat16),
            pltpu.VMEM(shard, jnp.bfloat16),
            pltpu.VMEM((8 * PAIR, HEAD), jnp.float32),
            pltpu.VMEM((8 * PAIR, 2 * HEAD), jnp.float32),
            pltpu.VMEM((PAIR, widest), jnp.float32),
            pltpu.VMEM((PAIR, widest), jnp.float32),
            pltpu.VMEM((PAIR, HEAD), jnp.float32),
            pltpu.VMEM((PAIR, HEAD), jnp.float32),
            pltpu.VMEM(shard, jnp.bfloat16),
            pltpu.VMEM(shard, jnp.bfloat16),
        ]
        + [dma] * 6,
        compiler_params=pltpu.CompilerParams(
            collective_id=0, has_side_effects=True, vmem_limit_bytes=56 * 2**20
        ),
        cost_estimate=pl.CostEstimate(flops=8860000000, bytes_accessed=600000, transcendentals=17300000),
        name="attend",
    )(query, keys, values)


def solution(mesh):
    spec = P(("blk", "sp"), None)
    return jax.shard_map(local, mesh=mesh, in_specs=(spec, spec, spec), out_specs=spec, check_vma=False)
```
